128 devices in a mesh: gy: 8 (over y, core), gz: 16 (over x, z).
Axes of the slice: x: 4, y: 4, z: 4, core: 2. Of those that a mesh axis runs over, the one named last changes fastest.
Arguments:
- velocity: float32 [1536, 147456], P('gz', 'gy'), may hold values from -6 to 6
Outputs:
- deriv_y: float32 [1536, 147456], P('gz', 'gy')
- deriv_z: float32 [1536, 147456], P('gz', 'gy')
The draws below stay inside these ranges and needn't reach their ends.
All inputs are finite; a program needn't handle non-finite values.
Results may differ from the reference program's by a relative error of at most 0.00007.
Values sent between devices are 32-bit elements; how exact they have to be, the bound alone decides.
No kernel may reach another device: no remote copies, remote signals or barrier semaphores. Data moves between devices by JAX's collectives and lax.ppermute only.
A program may use at most 192 MiB of HBM per device.

```python
import jax
import jax.numpy as jnp
from jax import lax

X = 96
NY = 1536
NZ = 1536


def shard_levels(key, dims, pieces, smallest, largest):
    loudness, own = 1.0, jax.random.fold_in(key, 6)
    for position, parts in pieces:
        heights = jnp.exp(jax.random.uniform(jax.random.fold_in(own, position), (parts,), jnp.float32, smallest / len(pieces), largest / len(pieces)))
        loudness = loudness * jnp.repeat(heights, dims[position] // parts).reshape([-1 if axis == position else 1 for axis in range(len(dims))])
    return loudness


def centred(rng, dims, width, bound, cuts=(), kind=jnp.bfloat16):
    result = width * jax.random.normal(rng, dims, jnp.float32)
    if cuts:
        result = result * shard_levels(rng, dims, cuts, -0.22, 0.18)
    return jnp.clip(result, -bound, bound).astype(kind)


def setup_inputs(seed: int = 0) -> dict:
    streams_of = jax.random.split(jax.random.key(seed), 2)
    velocity = centred(streams_of[0], (NZ, NY * X), 1.0, 6.0, ((0, 16), (1, 8)), jnp.float32)
    return {"velocity": velocity}


COUPLING = 1.0 / 3.0
NEAR_COEF = 7.0 / 9.0
FAR_COEF = 1.0 / 36.0


def compact_along(values_in, axis_at):
    extent = values_in.shape[axis_at]
    source = NEAR_COEF * (jnp.roll(values_in, -1, axis_at) - jnp.roll(values_in, 1, axis_at))
    source = source + FAR_COEF * (jnp.roll(values_in, -2, axis_at) - jnp.roll(values_in, 2, axis_at))
    waves = jnp.arange(extent).astype(values_in.dtype)
    symbol = 1.0 + 2.0 * COUPLING * jnp.cos(2.0 * jnp.pi * waves / extent)
    layout = [1, 1]
    layout[axis_at] = extent
    spectrum = jnp.fft.fft(source, axis=axis_at) / symbol.reshape(layout)
    return jnp.real(jnp.fft.ifft(spectrum, axis=axis_at)).astype(values_in.dtype)


def one_plane(section):
    return compact_along(section, 1), compact_along(section, 0)


def reference(velocity):
    planes = jnp.transpose(velocity.reshape(NZ, NY, X), (2, 0, 1))
    deriv_y, deriv_z = lax.map(one_plane, planes)
    deriv_y = jnp.transpose(deriv_y, (1, 2, 0)).reshape(NZ, NY * X)
    deriv_z = jnp.transpose(deriv_z, (1, 2, 0)).reshape(NZ, NY * X)
    return deriv_y, deriv_z
```

```python
import functools

import jax
import jax.numpy as jnp
import ml_dtypes
import numpy as np
from jax import lax
from jax.experimental import pallas as pl
from jax.experimental.pallas import tpu as pltpu
from jax.sharding import PartitionSpec as P

X = 96
ROOT = (5.0**0.5 - 3.0) / 2.0
EDGE = 1.0 / 12.0
GAIN = 25.0 / 12.0
LANES = 128
BLOCK = 4 * X
Q = ROOT**4
F32 = jnp.float32


def lane_index(rows):
    return lax.broadcasted_iota(jnp.int32, (rows, LANES), 1)


def rolled(x, by):
    return pltpu.roll(x, by, 1)


def summarize(u_hbm, u_v, zf, zb, yf, yb, acc_f, acc_b, sems, *, chunks):
    rows, width = u_v.shape
    wide = width // chunks
    per = wide // BLOCK

    def copy(c):
        lanes = pl.ds(c * wide, wide)
        return pltpu.make_async_copy(u_hbm.at[:, lanes], u_v.at[:, lanes], sems.at[c])

    for c in range(chunks):
        copy(c).start()
    sub = lax.broadcasted_iota(jnp.int32, (8, wide), 0)
    w_f = jnp.zeros((8, wide), F32)
    w_b = jnp.zeros((8, wide), F32)
    for r in range(8):
        w_f = jnp.where(sub == r, np.float32(ROOT ** (7 - r)), w_f)
        w_b = jnp.where(sub == r, np.float32(ROOT**r), w_b)
    for c in range(chunks):
        copy(c).wait()
        z_f = z_b = None
        for g in range(rows // 8):
            rs = slice(8 * g, 8 * g + 8)
            x = u_v[rs, c * wide : (c + 1) * wide]
            if g == 0:
                z_f, z_b = x, x
            else:
                z_f = z_f * np.float32(ROOT**8) + x
                z_b = z_b + x * np.float32(ROOT ** (8 * g))
            parts = [x[:, b * BLOCK : (b + 1) * BLOCK] for b in range(per)]
            y_f = acc_f[rs, :] if c else None
            for part in parts:
                y_f = part if y_f is None else y_f * np.float32(Q) + part
            acc_f[rs, :] = y_f
            y_b = None
            for part in reversed(parts):
                y_b = part if y_b is None else y_b * np.float32(Q) + part
            acc_b[rs, :] = acc_b[rs, :] + y_b * np.float32(Q ** (per * c)) if c else y_b
        lanes = slice(c * wide, (c + 1) * wide)
        zf[0:1, lanes] = jnp.sum(z_f * w_f, axis=0, keepdims=True)
        zb[0:1, lanes] = jnp.sum(z_b * w_b, axis=0, keepdims=True)
        zf[1:2, lanes] = u_v[rows - 1 : rows, lanes]
        zb[1:2, lanes] = u_v[0:1, lanes]
    lane = lane_index(8)
    for g in range(rows // 8):
        rs = slice(8 * g, 8 * g + 8)
        v0, v1, v2 = (acc_f[rs, k * LANES : (k + 1) * LANES] for k in range(3))
        s = v2 + np.float32(ROOT) * jnp.where(lane < 96, rolled(v1, 96), rolled(v2, 96))
        s = s + np.float32(ROOT**2) * jnp.where(lane < 64, rolled(v0, 64), rolled(v1, 64))
        s = s + np.float32(ROOT**3) * rolled(v0, 32)
        yf[rs, 0:LANES] = jnp.where(lane < 32, np.float32(0), s)
        yf[rs, LANES:] = u_v[rs, width - LANES :]
        v0, v1, v2 = (acc_b[rs, k * LANES : (k + 1) * LANES] for k in range(3))
        s = v0 + np.float32(ROOT) * jnp.where(lane < 32, rolled(v0, 32), rolled(v1, 32))
        s = s + np.float32(ROOT**2) * jnp.where(lane < 64, rolled(v1, 64), rolled(v2, 64))
        s = s + np.float32(ROOT**3) * rolled(v2, 96)
        yb[rs, 0:LANES] = jnp.where(lane < 96, s, np.float32(0))
        yb[rs, LANES:] = u_v[rs, 0:LANES]


def add(a, b):
    return b if a is None else a if b is None else a + b


def sub(a, b):
    return a if b is None else -b if a is None else a - b


def times(a, k):
    return None if a is None else a * np.float32(k)


def derive_y(u_v, low, high, dy, ybuf, obuf, sems, *, tall):
    rows, width = u_v.shape
    count = width // LANES
    lane = lane_index(tall)
    scale = GAIN * Q

    def step(i, carry):
        rs = pl.ds(pl.multiple_of(i * tall, tall), tall)
        s_low, s_high = low[rs, 0:LANES], high[rs, 0:LANES]
        t_low, t_high = low[rs, LANES:], high[rs, LANES:]

        @functools.cache
        def u(t):
            if 0 <= t < count:
                return u_v[rs, t * LANES : (t + 1) * LANES]
            return s_low if t == -1 else s_high if t == count else None

        @functools.cache
        def turn(t, by):
            return None if u(t) is None else rolled(u(t), by)

        def merge(below, a, b):
            if a is None and b is None:
                return None
            zero = jnp.zeros((tall, LANES), F32)
            return jnp.where(lane < below, zero if a is None else a, zero if b is None else b)

        @functools.cache
        def u1(t):
            return merge(96, turn(t - 1, 96), turn(t, 96))

        @functools.cache
        def u2(t):
            return merge(64, turn(t - 2, 64), turn(t - 1, 64))

        @functools.cache
        def u3(t):
            return merge(32, turn(t - 3, 32), turn(t - 2, 32))

        y = {-4: times(s_low, -scale)}
        for t in range(-3, count + 3):
            d1 = sub(u3(t + 3), u1(t))
            d2 = sub(u2(t + 3), u2(t))
            d3 = sub(u1(t + 3), u3(t))
            d4 = sub(u(t + 3), u(t - 3))
            f = sub(times(d1, 18 * scale), times(d2, 7 * scale))
            f = sub(add(f, times(d3, 3 * scale)), times(d4, scale))
            y[t] = add(f, times(y.pop(t - 3, None), Q))
            if 0 <= t < count:
                ybuf[:, t * LANES : (t + 1) * LANES] = y[t]
                if t == 0:
                    d1 = u3(t + 3) - jnp.where(lane < 96, rolled(t_low, 96), turn(t, 96))
                if t == count - 1:
                    d1 = jnp.where(lane < 32, turn(t, 32), rolled(t_high, 32)) - u1(t)
                obuf[rs, t * LANES : (t + 1) * LANES] = d1 * np.float32(EDGE)
        z = {}
        for k in range(3):
            tail = times(y[count + k], Q)
            if k == 0:
                tail = tail + s_high * np.float32(scale)
            z[count + k] = y[count + k] + tail * np.float32(Q / (1 - Q * Q))
        for t in reversed(range(count)):
            ls = slice(t * LANES, (t + 1) * LANES)
            z[t] = ybuf[:, ls] + z.pop(t + 3) * np.float32(Q)
            obuf[rs, ls] = obuf[rs, ls] + z[t]
        pltpu.make_async_copy(obuf.at[rs], dy.at[rs], sems.at[i]).start()
        return carry

    lax.fori_loop(0, rows // tall, step, 0)

    def finish(i, carry):
        rs = pl.ds(pl.multiple_of(i * tall, tall), tall)
        pltpu.make_async_copy(obuf.at[rs], dy.at[rs], sems.at[i]).wait()
        return carry

    lax.fori_loop(0, rows // tall, finish, 0)


def halves(x):
    high = x.astype(jnp.bfloat16)
    return high, (x - high.astype(F32)).astype(jnp.bfloat16)


def z_matrix(rows):
    at = np.arange(rows)
    k = at[:, None] - at[None, :]
    own = GAIN * np.sign(k) * ROOT ** np.abs(k) - EDGE * ((k == 1).astype(float) - (k == -1))
    halo = np.zeros((rows, 16))
    halo[:, 0] = GAIN * ROOT ** (at + 1.0)
    halo[0, 1] = -EDGE
    halo[:, 2] = -GAIN * ROOT ** (rows - at * 1.0)
    halo[rows - 1, 3] = EDGE
    whole = np.concatenate([own, own, halo, halo], axis=1).astype(np.float32)
    high = whole.astype(ml_dtypes.bfloat16)
    low = (whole - high.astype(np.float32)).astype(ml_dtypes.bfloat16)
    return np.concatenate([high, low], axis=0)


def derive_z(u_v, low, high, matrix, dz, rhs, halo, obuf, sems, *, chunks):
    rows, width = u_v.shape
    wide = width // chunks
    halo[...] = jnp.zeros(halo.shape, F32)

    def step(i, carry):
        ls = pl.ds(pl.multiple_of(i * wide, wide), wide)
        halo[0:2, :] = low[:, ls]
        halo[2:4, :] = high[:, ls]
        rhs[0:rows, :], rhs[rows : 2 * rows, :] = halves(u_v[:, ls])
        rhs[2 * rows : 2 * rows + 16, :], rhs[2 * rows + 16 :, :] = halves(halo[...])
        out = jnp.dot(matrix[...], rhs[...], preferred_element_type=F32)
        obuf[:, ls] = out[:rows] + out[rows:]
        pltpu.make_async_copy(obuf.at[:, ls], dz.at[:, ls], sems.at[i]).start()
        return carry

    lax.fori_loop(0, chunks, step, 0)

    def finish(i, carry):
        ls = pl.ds(pl.multiple_of(i * wide, wide), wide)
        pltpu.make_async_copy(obuf.at[:, ls], dz.at[:, ls], sems.at[i]).wait()
        return carry

    lax.fori_loop(0, chunks, finish, 0)


VMEM = pl.BlockSpec(memory_space=pltpu.VMEM)
ANY = pl.BlockSpec(memory_space=pl.ANY)
PARAMS = pltpu.CompilerParams(vmem_limit_bytes=44 * 1024 * 1024)


def shards(velocity):
    rows, width = velocity.shape
    chunks = 12
    u_v, zf, zb, yf, yb = pl.pallas_call(
        functools.partial(summarize, chunks=chunks),
        out_shape=(
            pltpu.VMEM((rows, width), F32),
            jax.ShapeDtypeStruct((2, width), F32),
            jax.ShapeDtypeStruct((2, width), F32),
            jax.ShapeDtypeStruct((rows, 2 * LANES), F32),
            jax.ShapeDtypeStruct((rows, 2 * LANES), F32),
        ),
        in_specs=[ANY],
        out_specs=(VMEM,) * 5,
        scratch_shapes=[
            pltpu.VMEM((rows, BLOCK), F32),
            pltpu.VMEM((rows, BLOCK), F32),
            pltpu.SemaphoreType.DMA((chunks,)),
        ],
        compiler_params=PARAMS,
        name="summarize",
    )(velocity)

    def ring(axis, step):
        count = lax.axis_size(axis)
        return [(i, (i + step) % count) for i in range(count)]

    z_low = lax.ppermute(zf, "gz", ring("gz", 1))
    z_high = lax.ppermute(zb, "gz", ring("gz", -1))
    y_low = lax.ppermute(yf, "gy", ring("gy", 1))
    y_high = lax.ppermute(yb, "gy", ring("gy", -1))
    whole = jax.ShapeDtypeStruct((rows, width), F32)
    tall = 16
    dy = pl.pallas_call(
        functools.partial(derive_y, tall=tall),
        out_shape=whole,
        in_specs=[VMEM] * 3,
        out_specs=ANY,
        scratch_shapes=[
            pltpu.VMEM((tall, width), F32),
            pltpu.VMEM((rows, width), F32),
            pltpu.SemaphoreType.DMA((rows // tall,)),
        ],
        compiler_params=PARAMS,
        cost_estimate=pl.CostEstimate(flops=8_000_000, bytes_accessed=14_000_000, transcendentals=0),
        name="derive_y",
    )(pltpu.with_memory_space_constraint(u_v, pltpu.VMEM), y_low, y_high)
    dz = pl.pallas_call(
        functools.partial(derive_z, chunks=chunks),
        out_shape=whole,
        in_specs=[VMEM] * 4,
        out_specs=ANY,
        scratch_shapes=[
            pltpu.VMEM((2 * rows + 32, width // chunks), jnp.bfloat16),
            pltpu.VMEM((16, width // chunks), F32),
            pltpu.VMEM((rows, width), F32),
            pltpu.SemaphoreType.DMA((chunks,)),
        ],
        compiler_params=PARAMS,
        cost_estimate=pl.CostEstimate(flops=8_000_000, bytes_accessed=7_000_000, transcendentals=0),
        name="derive_z",
    )(pltpu.with_memory_space_constraint(u_v, pltpu.VMEM), z_low, z_high, jnp.asarray(z_matrix(rows)))
    return dy, dz


def solution(mesh):
    return jax.shard_map(
        shards,
        mesh=mesh,
        in_specs=(P("gz", "gy"),),
        out_specs=(P("gz", "gy"), P("gz", "gy")),
        check_vma=False,
    )
```

```python
import functools

import jax
import jax.numpy as jnp
import ml_dtypes
import numpy as np
from jax import lax
from jax.experimental import pallas as pl
from jax.experimental.pallas import tpu as pltpu
from jax.sharding import PartitionSpec as P

X = 96
ROOT = (5.0**0.5 - 3.0) / 2.0
EDGE = 1.0 / 12.0
GAIN = 25.0 / 12.0
LANES = 128
BLOCK = 4 * X
Q = ROOT**4
F32 = jnp.float32


def lane_index(rows):
    return lax.broadcasted_iota(jnp.int32, (rows, LANES), 1)


def rolled(x, by):
    return pltpu.roll(x, by, 1)


def is_even(axis):
    return lax.rem(lax.axis_index(axis), 2) == 0


def summarize(u_hbm, u_v, z0, z1, y0, y1, acc_f, acc_b, sems, *, chunks):
    rows, width = u_v.shape
    wide = width // chunks
    per = wide // BLOCK
    even_z, even_y = is_even("gz"), is_even("gy")

    def copy(c):
        lanes = pl.ds(c * wide, wide)
        return pltpu.make_async_copy(u_hbm.at[:, lanes], u_v.at[:, lanes], sems.at[c])

    for c in range(chunks):
        copy(c).start()
    sub = lax.broadcasted_iota(jnp.int32, (8, wide), 0)
    w_f = jnp.zeros((8, wide), F32)
    w_b = jnp.zeros((8, wide), F32)
    for r in range(8):
        w_f = jnp.where(sub == r, np.float32(ROOT ** (7 - r)), w_f)
        w_b = jnp.where(sub == r, np.float32(ROOT**r), w_b)
    for c in range(chunks):
        copy(c).wait()
        z_f = z_b = None
        for g in range(rows // 8):
            rs = slice(8 * g, 8 * g + 8)
            x = u_v[rs, c * wide : (c + 1) * wide]
            if g == 0:
                z_f, z_b = x, x
            else:
                z_f = z_f * np.float32(ROOT**8) + x
                z_b = z_b + x * np.float32(ROOT ** (8 * g))
            parts = [x[:, b * BLOCK : (b + 1) * BLOCK] for b in range(per)]
            y_f = acc_f[rs, :] if c else None
            for part in parts:
                y_f = part if y_f is None else y_f * np.float32(Q) + part
            acc_f[rs, :] = y_f
            y_b = None
            for part in reversed(parts):
                y_b = part if y_b is None else y_b * np.float32(Q) + part
            acc_b[rs, :] = acc_b[rs, :] + y_b * np.float32(Q ** (per * c)) if c else y_b
        lanes = slice(c * wide, (c + 1) * wide)
        s_f = jnp.sum(z_f * w_f, axis=0, keepdims=True)
        s_b = jnp.sum(z_b * w_b, axis=0, keepdims=True)
        e_f, e_b = u_v[rows - 1 : rows, lanes], u_v[0:1, lanes]
        z0[0:1, lanes] = jnp.where(even_z, s_f, s_b)
        z1[0:1, lanes] = jnp.where(even_z, s_b, s_f)
        z0[1:2, lanes] = jnp.where(even_z, e_f, e_b)
        z1[1:2, lanes] = jnp.where(even_z, e_b, e_f)
    lane = lane_index(8)
    for g in range(rows // 8):
        rs = slice(8 * g, 8 * g + 8)
        v0, v1, v2 = (acc_f[rs, k * LANES : (k + 1) * LANES] for k in range(3))
        s = v2 + np.float32(ROOT) * jnp.where(lane < 96, rolled(v1, 96), rolled(v2, 96))
        s = s + np.float32(ROOT**2) * jnp.where(lane < 64, rolled(v0, 64), rolled(v1, 64))
        s = s + np.float32(ROOT**3) * rolled(v0, 32)
        s_f, e_f = rolled(s, 96), rolled(u_v[rs, width - LANES :], 96)
        v0, v1, v2 = (acc_b[rs, k * LANES : (k + 1) * LANES] for k in range(3))
        s = v0 + np.float32(ROOT) * jnp.where(lane < 32, rolled(v0, 32), rolled(v1, 32))
        s = s + np.float32(ROOT**2) * jnp.where(lane < 64, rolled(v1, 64), rolled(v2, 64))
        s_b, e_b = s + np.float32(ROOT**3) * rolled(v2, 96), u_v[rs, 0:LANES]
        y0[rs, 0:LANES] = jnp.where(even_y, s_f, s_b)
        y1[rs, 0:LANES] = jnp.where(even_y, s_b, s_f)
        y0[rs, LANES:] = jnp.where(even_y, e_f, e_b)
        y1[rs, LANES:] = jnp.where(even_y, e_b, e_f)


def halves(x):
    high = x.astype(jnp.bfloat16)
    return high, (x - high.astype(F32)).astype(jnp.bfloat16)


def z_matrix(rows):
    at = np.arange(rows)
    k = at[:, None] - at[None, :]
    own = GAIN * np.sign(k) * ROOT ** np.abs(k) - EDGE * ((k == 1).astype(float) - (k == -1))
    whole = np.concatenate([own, own], axis=1).astype(np.float32)
    high = whole.astype(ml_dtypes.bfloat16)
    low = (whole - high.astype(np.float32)).astype(ml_dtypes.bfloat16)
    return np.concatenate([high, low], axis=0)


def local(u_v, matrix, z_own, v, rhs, *, chunks):
    rows, width = u_v.shape
    wide = width // chunks
    per = wide // BLOCK
    part = 48

    def step(c, carry):
        start = pl.multiple_of(c * wide, wide)
        ls = pl.ds(start, wide)
        rhs[0:rows, :], rhs[rows:, :] = halves(u_v[:, ls])
        out = jnp.dot(matrix[...], rhs[...], preferred_element_type=F32)
        z_own[:, ls] = out[:rows] + out[rows:]
        lane = lane_index(part)
        keep_low = jnp.where(c > 0, np.float32(EDGE), np.float32(0))
        keep_high = jnp.where(c < chunks - 1, np.float32(EDGE), np.float32(0))
        below = pl.multiple_of(jnp.maximum(start - LANES, 0), LANES)
        above = pl.multiple_of(jnp.minimum(start + wide, width - LANES), LANES)
        for r in range(0, rows, part):
            rs = slice(r, r + part)
            before = rolled(u_v[rs, pl.ds(below, LANES)] * keep_low, 96)
            points = []
            for b in range(per):
                at = start + b * BLOCK
                v0, v1, v2 = (
                    u_v[rs, pl.ds(pl.multiple_of(at + k * LANES, LANES), LANES)] * np.float32(EDGE) for k in range(3)
                )
                points += [
                    v0,
                    jnp.where(lane < 32, rolled(v0, 32), rolled(v1, 32)),
                    jnp.where(lane < 64, rolled(v1, 64), rolled(v2, 64)),
                    rolled(v2, 96),
                ]
            points.append(u_v[rs, pl.ds(above, LANES)] * keep_high)
            points = [before] + points
            for j in range(4 * per):
                v[4 * per * c + j, rs, :] = points[j + 2] - points[j]
        return carry

    lax.fori_loop(0, chunks, step, 0)


def finish(u_v, z_own, v, z0, z1, y0, y1, dy, dz, y, dy_v, dz_v, sem_y, sem_z, *, chunks):
    rows, width = u_v.shape
    points = v.shape[0]
    wide = width // chunks
    per = wide // BLOCK
    even_z, even_y = is_even("gz"), is_even("gy")

    def copy_z(c):
        ls = pl.ds(pl.multiple_of(c * wide, wide), wide)
        return pltpu.make_async_copy(dz_v.at[:, ls], dz.at[:, ls], sem_z.at[c])

    def copy_y(c):
        ls = pl.ds(pl.multiple_of(c * wide, wide), wide)
        return pltpu.make_async_copy(dy_v.at[:, ls], dy.at[:, ls], sem_y.at[c])

    row = lax.broadcasted_iota(jnp.int32, (8, 3 * LANES), 0)
    w_low = jnp.zeros((8, 3 * LANES), F32)
    w_high = jnp.zeros((8, 3 * LANES), F32)
    for r in range(8):
        w_low = jnp.where(row == r, np.float32(GAIN * ROOT ** (r + 1)), w_low)
        w_high = jnp.where(row == r, np.float32(-GAIN * ROOT ** (8 - r)), w_high)

    def z_step(c, carry):
        for k in range(wide // (3 * LANES)):
            ls = pl.ds(pl.multiple_of(c * wide + k * 3 * LANES, 3 * LANES), 3 * LANES)
            first, second = z0[:, ls], z1[:, ls]
            low = jnp.where(even_z, second, first)
            high = jnp.where(even_z, first, second)
            t_low, t_high = low[0:1] * w_low, high[0:1] * w_high
            for g in range(rows // 8):
                rs = slice(8 * g, 8 * g + 8)
                d = z_own[rs, ls] + t_low * np.float32(ROOT ** (8 * g))
                d = d + t_high * np.float32(ROOT ** (rows - 8 - 8 * g))
                if g == 0:
                    d = d - jnp.where(row == 0, np.float32(EDGE) * low[1:2], np.float32(0))
                if g == rows // 8 - 1:
                    d = d + jnp.where(row == 7, np.float32(EDGE) * high[1:2], np.float32(0))
                dz_v[rs, ls] = d
        copy_z(c).start()
        return carry

    lax.fori_loop(0, chunks, z_step, 0)

    tall = lane_index(rows)
    y_low = jnp.where(even_y, y1[...], y0[...]) * np.float32(EDGE)
    y_high = jnp.where(even_y, y0[...], y1[...]) * np.float32(EDGE)
    s_low, s_high = y_low[:, :LANES], y_high[:, :LANES]
    state = u_v[:, 0:LANES] * np.float32(EDGE) + s_low * np.float32(ROOT - 1 / ROOT)

    def forward(i, state):
        for k in range(4):
            state = v[4 * i + k] + state * np.float32(ROOT)
            y[4 * i + k] = state
        return state

    state = lax.fori_loop(0, points // 4, forward, state) + s_high
    y[points - 1] = state
    u_last = rolled(u_v[:, width - LANES :], 96) * np.float32(EDGE)
    after = state * np.float32(ROOT) - u_last
    far = after * np.float32(ROOT) - s_high
    state = after + far * np.float32(ROOT / (1 - ROOT * ROOT))

    def backward(i, state):
        c = chunks - 1 - i
        part = 48
        state = list(state)
        for b in reversed(range(per)):
            for h in range(rows // part):
                rs = slice(h * part, (h + 1) * part)
                d = [None] * 4
                for k in reversed(range(4)):
                    j = 4 * (per * c + b) + k
                    state[h] = y[j, rs, :] + state[h] * np.float32(ROOT)
                    d[k] = v[j, rs, :] + state[h] * np.float32(-25 * ROOT)
                lane = lane_index(part)
                d1, d2, d3 = rolled(d[1], 96), rolled(d[2], 64), rolled(d[3], 32)
                at = c * wide + b * BLOCK
                for k, o in enumerate((jnp.where(lane < 96, d[0], d1), jnp.where(lane < 64, d1, d2), jnp.where(lane < 32, d2, d3))):
                    dy_v[rs, pl.ds(pl.multiple_of(at + k * LANES, LANES), LANES)] = o

        @pl.when(i == 0)
        def _():
            edge = rolled(y_high[:, LANES:], 32)
            dy_v[:, width - LANES :] = dy_v[:, width - LANES :] + jnp.where(tall < 32, np.float32(0), edge)

        @pl.when(i == chunks - 1)
        def _():
            dy_v[:, 0:LANES] = dy_v[:, 0:LANES] - jnp.where(tall < 96, y_low[:, LANES:], np.float32(0))

        copy_y(c).start()
        return tuple(state)

    lax.fori_loop(0, chunks, backward, (state[:48], state[48:]))

    def wait(c, carry):
        copy_z(c).wait()
        copy_y(c).wait()
        return carry

    lax.fori_loop(0, chunks, wait, 0)


VMEM = pl.BlockSpec(memory_space=pltpu.VMEM)
ANY = pl.BlockSpec(memory_space=pl.ANY)


def params(mib):
    return pltpu.CompilerParams(vmem_limit_bytes=mib * 1024 * 1024)


def here(x):
    return pltpu.with_memory_space_constraint(x, pltpu.VMEM)


def shards(velocity):
    rows, width = velocity.shape
    points = width // X
    chunks = 12
    whole = jax.ShapeDtypeStruct((rows, width), F32)
    u_v, z0, z1, y0, y1 = pl.pallas_call(
        functools.partial(summarize, chunks=chunks),
        out_shape=(
            pltpu.VMEM((rows, width), F32),
            jax.ShapeDtypeStruct((2, width), F32),
            jax.ShapeDtypeStruct((2, width), F32),
            jax.ShapeDtypeStruct((rows, 2 * LANES), F32),
            jax.ShapeDtypeStruct((rows, 2 * LANES), F32),
        ),
        in_specs=[ANY],
        out_specs=(VMEM,) * 5,
        scratch_shapes=[
            pltpu.VMEM((rows, BLOCK), F32),
            pltpu.VMEM((rows, BLOCK), F32),
            pltpu.SemaphoreType.DMA((chunks,)),
        ],
        compiler_params=params(12),
        name="summarize",
    )(pltpu.with_memory_space_constraint(velocity, pltpu.HBM))

    def swap(x, axis, first):
        count = lax.axis_size(axis)
        pairs = [(i % count, (i + 1) % count) for i in range(first, count + first, 2)]
        return lax.ppermute(x, axis, pairs + [(b, a) for a, b in pairs])

    z0, z1 = swap(z0, "gz", 0), swap(z1, "gz", 1)
    y0, y1 = swap(y0, "gy", 0), swap(y1, "gy", 1)
    z_own, v = pl.pallas_call(
        functools.partial(local, chunks=chunks),
        out_shape=(pltpu.VMEM((rows, width), F32), pltpu.VMEM((points, rows, LANES), F32)),
        in_specs=[VMEM] * 2,
        out_specs=(VMEM,) * 2,
        scratch_shapes=[pltpu.VMEM((2 * rows, width // chunks), jnp.bfloat16)],
        compiler_params=params(8),
        cost_estimate=pl.CostEstimate(flops=8_000_000, bytes_accessed=10_000_000, transcendentals=0),
        name="local",
    )(here(u_v), jnp.asarray(z_matrix(rows)))
    return pl.pallas_call(
        functools.partial(finish, chunks=chunks),
        out_shape=(whole, whole),
        in_specs=[VMEM] * 7,
        out_specs=(ANY, ANY),
        scratch_shapes=[
            pltpu.VMEM((points, rows, LANES), F32),
            pltpu.VMEM((rows, width), F32),
            pltpu.VMEM((rows, width), F32),
            pltpu.SemaphoreType.DMA((chunks,)),
            pltpu.SemaphoreType.DMA((chunks,)),
        ],
        compiler_params=params(26),
        cost_estimate=pl.CostEstimate(flops=8_000_000, bytes_accessed=14_000_000, transcendentals=0),
        name="finish",
    )(here(u_v), here(z_own), here(v), z0, z1, y0, y1)


def solution(mesh):
    return jax.shard_map(
        shards,
        mesh=mesh,
        in_specs=(P("gz", "gy"),),
        out_specs=(P("gz", "gy"), P("gz", "gy")),
        check_vma=False,
    )
```

```python
import functools

import jax
import jax.numpy as jnp
import ml_dtypes
import numpy as np
from jax import lax
from jax.experimental import pallas as pl
from jax.experimental.pallas import tpu as pltpu
from jax.sharding import PartitionSpec as P

X = 96
ROOT = (5.0**0.5 - 3.0) / 2.0
EDGE = 1.0 / 12.0
GAIN = 25.0 / 12.0
LANES = 128
BLOCK = 4 * X
Q = ROOT**4
UL = 2
UF = 4
FORWARD = 48
F32 = jnp.float32


def lane_index(rows):
    return lax.broadcasted_iota(jnp.int32, (rows, LANES), 1)


def rolled(x, by):
    return pltpu.roll(x, by, 1)


def is_even(axis):
    return lax.rem(lax.axis_index(axis), 2) == 0


def summarize(u_hbm, u_v, z0, z1, y0, y1, acc_f, acc_b, sems, *, chunks):
    rows, width = u_v.shape
    wide = width // chunks
    per = wide // BLOCK
    even_z, even_y = is_even("gz"), is_even("gy")

    def copy(c):
        lanes = pl.ds(c * wide, wide)
        return pltpu.make_async_copy(u_hbm.at[:, lanes], u_v.at[:, lanes], sems.at[c])

    for c in range(chunks):
        copy(c).start()
    sub = lax.broadcasted_iota(jnp.int32, (8, wide), 0)
    w_f = jnp.zeros((8, wide), F32)
    w_b = jnp.zeros((8, wide), F32)
    for r in range(8):
        w_f = jnp.where(sub == r, np.float32(ROOT ** (7 - r)), w_f)
        w_b = jnp.where(sub == r, np.float32(ROOT**r), w_b)
    for c in range(chunks):
        copy(c).wait()
        z_f = z_b = None
        for g in range(rows // 8):
            rs = slice(8 * g, 8 * g + 8)
            x = u_v[rs, c * wide : (c + 1) * wide]
            if g == 0:
                z_f, z_b = x, x
            else:
                z_f = z_f * np.float32(ROOT**8) + x
                z_b = z_b + x * np.float32(ROOT ** (8 * g))
            parts = [x[:, b * BLOCK : (b + 1) * BLOCK] for b in range(per)]
            y_f = acc_f[rs, :] if c else None
            for part in parts:
                y_f = part if y_f is None else y_f * np.float32(Q) + part
            acc_f[rs, :] = y_f
            y_b = None
            for part in reversed(parts):
                y_b = part if y_b is None else y_b * np.float32(Q) + part
            acc_b[rs, :] = acc_b[rs, :] + y_b * np.float32(Q ** (per * c)) if c else y_b
        lanes = slice(c * wide, (c + 1) * wide)
        s_f = jnp.sum(z_f * w_f, axis=0, keepdims=True)
        s_b = jnp.sum(z_b * w_b, axis=0, keepdims=True)
        e_f, e_b = u_v[rows - 1 : rows, lanes], u_v[0:1, lanes]
        z0[0:1, lanes] = jnp.where(even_z, s_f, s_b)
        z1[0:1, lanes] = jnp.where(even_z, s_b, s_f)
        z0[1:2, lanes] = jnp.where(even_z, e_f, e_b)
        z1[1:2, lanes] = jnp.where(even_z, e_b, e_f)
    lane = lane_index(8)
    for g in range(rows // 8):
        rs = slice(8 * g, 8 * g + 8)
        v0, v1, v2 = (acc_f[rs, k * LANES : (k + 1) * LANES] for k in range(3))
        s = v2 + np.float32(ROOT) * jnp.where(lane < 96, rolled(v1, 96), rolled(v2, 96))
        s = s + np.float32(ROOT**2) * jnp.where(lane < 64, rolled(v0, 64), rolled(v1, 64))
        s = s + np.float32(ROOT**3) * rolled(v0, 32)
        s_f, e_f = rolled(s, 96), rolled(u_v[rs, width - LANES :], 96)
        v0, v1, v2 = (acc_b[rs, k * LANES : (k + 1) * LANES] for k in range(3))
        s = v0 + np.float32(ROOT) * jnp.where(lane < 32, rolled(v0, 32), rolled(v1, 32))
        s = s + np.float32(ROOT**2) * jnp.where(lane < 64, rolled(v1, 64), rolled(v2, 64))
        s_b, e_b = s + np.float32(ROOT**3) * rolled(v2, 96), u_v[rs, 0:LANES]
        y0[rs, 0:LANES] = jnp.where(even_y, s_f, s_b)
        y1[rs, 0:LANES] = jnp.where(even_y, s_b, s_f)
        y0[rs, LANES:] = jnp.where(even_y, e_f, e_b)
        y1[rs, LANES:] = jnp.where(even_y, e_b, e_f)


def halves(x):
    high = x.astype(jnp.bfloat16)
    return high, (x - high.astype(F32)).astype(jnp.bfloat16)


def z_matrix(rows):
    at = np.arange(rows)
    k = at[:, None] - at[None, :]
    own = GAIN * np.sign(k) * ROOT ** np.abs(k) - EDGE * ((k == 1).astype(float) - (k == -1))
    whole = np.concatenate([own, own], axis=1).astype(np.float32)
    high = whole.astype(ml_dtypes.bfloat16)
    low = (whole - high.astype(np.float32)).astype(ml_dtypes.bfloat16)
    return np.concatenate([high, low], axis=0)


def local(u_v, matrix, z_own, v, rhs, last, *, chunks, unroll):
    rows, width = u_v.shape
    wide = width // chunks
    per = wide // BLOCK
    part = rows // 4
    lane = lane_index(part)
    last[...] = jnp.zeros((rows, LANES), F32)

    for c in range(chunks):
        ls = slice(c * wide, (c + 1) * wide)
        slot = c % unroll
        rhs[slot, 0:rows, :], rhs[slot, rows:, :] = halves(u_v[:, ls])
        out = jnp.dot(matrix[...], rhs[slot], preferred_element_type=F32)
        z_own[:, ls] = out[:rows] + out[rows:]
        for r in range(0, rows, part):
            rs = slice(r, r + part)
            points = [last[rs, :]]
            for b in range(per):
                at = c * wide + b * BLOCK
                v0, v1, v2 = (u_v[rs, at + k * LANES : at + (k + 1) * LANES] * np.float32(EDGE) for k in range(3))
                points += [
                    v0,
                    rolled(jnp.where(lane < 96, v1, v0), 32),
                    rolled(jnp.where(lane < 64, v2, v1), 64),
                    rolled(v2, 96),
                ]
            last[rs, :] = points[-1]
            if c < chunks - 1:
                points.append(u_v[rs, (c + 1) * wide : (c + 1) * wide + LANES] * np.float32(EDGE))
            else:
                points.append(jnp.zeros((part, LANES), F32))
            for k in range(4 * per):
                v[4 * per * c + k, rs, :] = points[k + 2] - points[k]


def halo_matrix(rows):
    at = np.arange(rows)
    whole = np.zeros((rows, 8))
    whole[:, 0] = GAIN * ROOT ** (at + 1.0)
    whole[0, 1] = -EDGE
    whole[:, 2] = -GAIN * ROOT ** (rows - at * 1.0)
    whole[rows - 1, 3] = EDGE
    whole = whole.astype(np.float32)
    high = whole.astype(ml_dtypes.bfloat16)
    low = (whole - high.astype(np.float32)).astype(ml_dtypes.bfloat16)
    return np.concatenate([high, high, low, low], axis=1)


def finish(u_v, z_own, v, matrix, z0, z1, y0, y1, dy, dz, y, dy_v, dz_v, halo, rhs, sem_y, sem_z, *, chunks, unroll):
    rows, width = u_v.shape
    points = v.shape[0]
    wide = width // chunks
    per = wide // BLOCK
    even_z, even_y = is_even("gz"), is_even("gy")

    def copy(buffer, out, sems, c):
        ls = pl.ds(pl.multiple_of(c * wide, wide), wide)
        return pltpu.make_async_copy(buffer.at[:, ls], out.at[:, ls], sems.at[c])

    halo[...] = jnp.zeros(halo.shape, F32)

    def z_step(i, carry):
        for s in range(unroll):
            c = i * unroll + s
            slot = s
            ls = pl.ds(pl.multiple_of(c * wide, wide), wide)
            first, second = z0[:, ls], z1[:, ls]
            halo[slot, 0:2, :] = jnp.where(even_z, second, first)
            halo[slot, 2:4, :] = jnp.where(even_z, first, second)
            h = halo[slot]
            high = h.astype(jnp.bfloat16).astype(F32)
            both = jnp.concatenate([high, h - high], axis=0).astype(jnp.bfloat16)
            rhs[slot, 0:16, :] = both
            rhs[slot, 16:32, :] = both
            dz_v[:, ls] = z_own[:, ls] + jnp.dot(matrix[...], rhs[slot], preferred_element_type=F32)
            copy(dz_v, dz, sem_z, c).start()
        return carry

    lax.fori_loop(0, chunks // unroll, z_step, 0)

    y_low = jnp.where(even_y, y1[...], y0[...]) * np.float32(EDGE)
    y_high = jnp.where(even_y, y0[...], y1[...]) * np.float32(EDGE)
    s_low, s_high = y_low[:, :LANES], y_high[:, :LANES]
    state = u_v[:, 0:LANES] * np.float32(EDGE) + s_low * np.float32(ROOT - 1 / ROOT)

    def forward(i, state):
        for k in range(FORWARD):
            j = FORWARD * i + k
            state = v[j] + state * np.float32(ROOT)
            y[j] = state
        return state

    state = lax.fori_loop(0, points // FORWARD, forward, state) + s_high
    y[points - 1] = state
    u_last = rolled(u_v[:, width - LANES :], 96) * np.float32(EDGE)
    after = state * np.float32(ROOT) - u_last
    far = after * np.float32(ROOT) - s_high
    state = after + far * np.float32(ROOT / (1 - ROOT * ROOT))
    part = rows // 2
    lane = lane_index(part)
    state = [state[:part], state[part:]]
    for c in reversed(range(chunks)):
        for b in reversed(range(per)):
            for h in range(rows // part):
                rs = slice(h * part, (h + 1) * part)
                d = [None] * 4
                for k in reversed(range(4)):
                    j = 4 * (per * c + b) + k
                    state[h] = y[j, rs, :] + state[h] * np.float32(ROOT)
                    d[k] = v[j, rs, :] + state[h] * np.float32(-25 * ROOT)
                    if j == points - 1:
                        d[k] = d[k] + y_high[rs, LANES:]
                    if j == 0:
                        d[k] = d[k] - y_low[rs, LANES:]
                d1, d2, d3 = rolled(d[1], 96), rolled(d[2], 64), rolled(d[3], 32)
                at = c * wide + b * BLOCK
                for k, o in enumerate((jnp.where(lane < 96, d[0], d1), jnp.where(lane < 64, d1, d2), jnp.where(lane < 32, d2, d3))):
                    dy_v[rs, at + k * LANES : at + (k + 1) * LANES] = o
        copy(dy_v, dy, sem_y, c).start()

    for c in range(chunks):
        copy(dz_v, dz, sem_z, c).wait()
        copy(dy_v, dy, sem_y, c).wait()


VMEM = pl.BlockSpec(memory_space=pltpu.VMEM)
ANY = pl.BlockSpec(memory_space=pl.ANY)


def params(mib):
    return pltpu.CompilerParams(vmem_limit_bytes=mib * 1024 * 1024)


def here(x):
    return pltpu.with_memory_space_constraint(x, pltpu.VMEM)


def shards(velocity):
    rows, width = velocity.shape
    points = width // X
    chunks = 12
    whole = jax.ShapeDtypeStruct((rows, width), F32)
    u_v, z0, z1, y0, y1 = pl.pallas_call(
        functools.partial(summarize, chunks=chunks),
        out_shape=(
            pltpu.VMEM((rows, width), F32),
            jax.ShapeDtypeStruct((2, width), F32),
            jax.ShapeDtypeStruct((2, width), F32),
            jax.ShapeDtypeStruct((rows, 2 * LANES), F32),
            jax.ShapeDtypeStruct((rows, 2 * LANES), F32),
        ),
        in_specs=[ANY],
        out_specs=(VMEM,) * 5,
        scratch_shapes=[
            pltpu.VMEM((rows, BLOCK), F32),
            pltpu.VMEM((rows, BLOCK), F32),
            pltpu.SemaphoreType.DMA((chunks,)),
        ],
        compiler_params=params(12),
        name="summarize",
    )(pltpu.with_memory_space_constraint(velocity, pltpu.HBM))

    def swap(x, axis, first):
        count = lax.axis_size(axis)
        pairs = [(i % count, (i + 1) % count) for i in range(first, count + first, 2)]
        return lax.ppermute(x, axis, pairs + [(b, a) for a, b in pairs])

    z1 = swap(z1, "gz", 1)
    z0 = swap(z0, "gz", 0)
    y0, y1 = swap(y0, "gy", 0), swap(y1, "gy", 1)
    z_own, v = pl.pallas_call(
        functools.partial(local, chunks=chunks, unroll=UL),
        out_shape=(pltpu.VMEM((rows, width), F32), pltpu.VMEM((points, rows, LANES), F32)),
        in_specs=[VMEM] * 2,
        out_specs=(VMEM,) * 2,
        scratch_shapes=[pltpu.VMEM((UL, 2 * rows, width // chunks), jnp.bfloat16), pltpu.VMEM((rows, LANES), F32)],
        compiler_params=params(8),
        cost_estimate=pl.CostEstimate(flops=8_000_000, bytes_accessed=10_000_000, transcendentals=0),
        name="local",
    )(here(u_v), jnp.asarray(z_matrix(rows)))
    return pl.pallas_call(
        functools.partial(finish, chunks=chunks, unroll=UF),
        out_shape=(whole, whole),
        in_specs=[VMEM] * 8,
        out_specs=(ANY, ANY),
        scratch_shapes=[
            pltpu.VMEM((points, rows, LANES), F32),
            pltpu.VMEM((rows, width), F32),
            pltpu.VMEM((rows, width), F32),
            pltpu.VMEM((UF, 8, width // chunks), F32),
            pltpu.VMEM((UF, 32, width // chunks), jnp.bfloat16),
            pltpu.SemaphoreType.DMA((chunks,)),
            pltpu.SemaphoreType.DMA((chunks,)),
        ],
        compiler_params=params(26),
        cost_estimate=pl.CostEstimate(flops=8_000_000, bytes_accessed=14_000_000, transcendentals=0),
        name="finish",
    )(here(u_v), here(z_own), here(v), jnp.asarray(halo_matrix(rows)), z0, z1, y0, y1)


def solution(mesh):
    return jax.shard_map(
        shards,
        mesh=mesh,
        in_specs=(P("gz", "gy"),),
        out_specs=(P("gz", "gy"), P("gz", "gy")),
        check_vma=False,
    )
```

```python
import functools

import jax
import jax.numpy as jnp
import ml_dtypes
import numpy as np
from jax import lax
from jax.experimental import pallas as pl
from jax.experimental.pallas import tpu as pltpu
from jax.sharding import PartitionSpec as P

X = 96
ROOT = (5.0**0.5 - 3.0) / 2.0
EDGE = 1.0 / 12.0
GAIN = 25.0 / 12.0
LANES = 128
BLOCK = 4 * X
Q = ROOT**4
UL = 2
UF = 4
FORWARD = 48
F32 = jnp.float32


def lane_index(rows):
    return lax.broadcasted_iota(jnp.int32, (rows, LANES), 1)


def rolled(x, by):
    return pltpu.roll(x, by, 1)


def is_even(axis):
    return lax.rem(lax.axis_index(axis), 2) == 0


def summarize(u_hbm, m_hbm, u_v, z0, z1, y0, y1, z_own, v, acc_f, acc_b, matrix, rhs, last, sems, *, chunks, unroll):
    rows, width = u_v.shape
    wide = width // chunks
    per = wide // BLOCK
    even_z, even_y = is_even("gz"), is_even("gy")

    def copy(c):
        lanes = pl.ds(c * wide, wide)
        return pltpu.make_async_copy(u_hbm.at[:, lanes], u_v.at[:, lanes], sems.at[c])

    for c in range(chunks):
        copy(c).start()
    fetch = pltpu.make_async_copy(m_hbm, matrix, sems.at[chunks])
    fetch.start()
    sub = lax.broadcasted_iota(jnp.int32, (8, wide), 0)
    w_f = jnp.zeros((8, wide), F32)
    w_b = jnp.zeros((8, wide), F32)
    for r in range(8):
        w_f = jnp.where(sub == r, np.float32(ROOT ** (7 - r)), w_f)
        w_b = jnp.where(sub == r, np.float32(ROOT**r), w_b)
    for c in range(chunks):
        copy(c).wait()
        z_f = z_b = None
        for g in range(rows // 8):
            rs = slice(8 * g, 8 * g + 8)
            x = u_v[rs, c * wide : (c + 1) * wide]
            if g == 0:
                z_f, z_b = x, x
            else:
                z_f = z_f * np.float32(ROOT**8) + x
                z_b = z_b + x * np.float32(ROOT ** (8 * g))
            parts = [x[:, b * BLOCK : (b + 1) * BLOCK] for b in range(per)]
            y_f = acc_f[rs, :] if c else None
            for part in parts:
                y_f = part if y_f is None else y_f * np.float32(Q) + part
            acc_f[rs, :] = y_f
            y_b = None
            for part in reversed(parts):
                y_b = part if y_b is None else y_b * np.float32(Q) + part
            acc_b[rs, :] = acc_b[rs, :] + y_b * np.float32(Q ** (per * c)) if c else y_b
        lanes = slice(c * wide, (c + 1) * wide)
        s_f = jnp.sum(z_f * w_f, axis=0, keepdims=True)
        s_b = jnp.sum(z_b * w_b, axis=0, keepdims=True)
        e_f, e_b = u_v[rows - 1 : rows, lanes], u_v[0:1, lanes]
        z0[0:1, lanes] = jnp.where(even_z, s_f, s_b)
        z1[0:1, lanes] = jnp.where(even_z, s_b, s_f)
        z0[1:2, lanes] = jnp.where(even_z, e_f, e_b)
        z1[1:2, lanes] = jnp.where(even_z, e_b, e_f)
    lane = lane_index(8)
    y1[rows:, :] = jnp.zeros((8, 2 * LANES), F32)
    for g in range(rows // 8):
        rs = slice(8 * g, 8 * g + 8)
        v0, v1, v2 = (acc_f[rs, k * LANES : (k + 1) * LANES] for k in range(3))
        s = v2 + np.float32(ROOT) * jnp.where(lane < 96, rolled(v1, 96), rolled(v2, 96))
        s = s + np.float32(ROOT**2) * jnp.where(lane < 64, rolled(v0, 64), rolled(v1, 64))
        s = s + np.float32(ROOT**3) * rolled(v0, 32)
        s_f, e_f = rolled(s, 96), rolled(u_v[rs, width - LANES :], 96)
        v0, v1, v2 = (acc_b[rs, k * LANES : (k + 1) * LANES] for k in range(3))
        s = v0 + np.float32(ROOT) * jnp.where(lane < 32, rolled(v0, 32), rolled(v1, 32))
        s = s + np.float32(ROOT**2) * jnp.where(lane < 64, rolled(v1, 64), rolled(v2, 64))
        s_b, e_b = s + np.float32(ROOT**3) * rolled(v2, 96), u_v[rs, 0:LANES]
        y0[rs, 0:LANES] = jnp.where(even_y, s_f, s_b)
        y1[rs, 0:LANES] = jnp.where(even_y, s_b, s_f)
        y0[rs, LANES:] = jnp.where(even_y, e_f, e_b)
        y1[rs, LANES:] = jnp.where(even_y, e_b, e_f)
    fetch.wait()

    @pl.when(at_wrap())
    def _():
        own_parts(u_v, matrix, z_own, v, rhs, last, chunks=chunks, unroll=unroll)


def halves(x):
    high = x.astype(jnp.bfloat16)
    return high, (x - high.astype(F32)).astype(jnp.bfloat16)


def z_matrix(rows):
    at = np.arange(rows)
    k = at[:, None] - at[None, :]
    own = GAIN * np.sign(k) * ROOT ** np.abs(k) - EDGE * ((k == 1).astype(float) - (k == -1))
    whole = np.concatenate([own, own], axis=1).astype(np.float32)
    high = whole.astype(ml_dtypes.bfloat16)
    low = (whole - high.astype(np.float32)).astype(ml_dtypes.bfloat16)
    return np.concatenate([high, low], axis=0)


def own_parts(u_v, matrix, z_own, v, rhs, last, *, chunks, unroll):
    rows, width = u_v.shape
    wide = width // chunks
    per = wide // BLOCK
    part = rows // 4
    lane = lane_index(part)
    last[...] = jnp.zeros((rows, LANES), F32)

    for c in range(chunks):
        ls = slice(c * wide, (c + 1) * wide)
        slot = c % unroll
        rhs[slot, 0:rows, :], rhs[slot, rows:, :] = halves(u_v[:, ls])
        out = jnp.dot(matrix[...], rhs[slot], preferred_element_type=F32)
        z_own[:, ls] = out[:rows] + out[rows:]
        for r in range(0, rows, part):
            rs = slice(r, r + part)
            points = [last[rs, :]]
            for b in range(per):
                at = c * wide + b * BLOCK
                v0, v1, v2 = (u_v[rs, at + k * LANES : at + (k + 1) * LANES] * np.float32(EDGE) for k in range(3))
                points += [
                    v0,
                    rolled(jnp.where(lane < 96, v1, v0), 32),
                    rolled(jnp.where(lane < 64, v2, v1), 64),
                    rolled(v2, 96),
                ]
            last[rs, :] = points[-1]
            if c < chunks - 1:
                points.append(u_v[rs, (c + 1) * wide : (c + 1) * wide + LANES] * np.float32(EDGE))
            else:
                points.append(jnp.zeros((part, LANES), F32))
            for k in range(4 * per):
                v[4 * per * c + k, rs, :] = points[k + 2] - points[k]


def at_wrap():
    return lax.axis_index("gz") == 0


def local(u_v, matrix, z_before, v_before, z_own, v, rhs, last, *, chunks, unroll):
    del z_before, v_before

    @pl.when(jnp.logical_not(at_wrap()))
    def _():
        own_parts(u_v, matrix, z_own, v, rhs, last, chunks=chunks, unroll=unroll)


def halo_matrix(rows):
    at = np.arange(rows)
    whole = np.zeros((rows, 8))
    whole[:, 0] = GAIN * ROOT ** (at + 1.0)
    whole[0, 1] = -EDGE
    whole[:, 2] = -GAIN * ROOT ** (rows - at * 1.0)
    whole[rows - 1, 3] = EDGE
    whole = whole.astype(np.float32)
    high = whole.astype(ml_dtypes.bfloat16)
    low = (whole - high.astype(np.float32)).astype(ml_dtypes.bfloat16)
    return np.concatenate([high, high, low, low], axis=1)


def finish(u_v, z_own, v, matrix, z0, z1, y0, y1, dy, dz, y, dy_v, dz_v, halo, rhs, sem_y, sem_z, *, chunks, unroll):
    rows, width = u_v.shape
    points = v.shape[0]
    wide = width // chunks
    per = wide // BLOCK
    even_z, even_y = is_even("gz"), is_even("gy")

    def copy(buffer, out, sems, c):
        ls = pl.ds(pl.multiple_of(c * wide, wide), wide)
        return pltpu.make_async_copy(buffer.at[:, ls], out.at[:, ls], sems.at[c])

    halo[...] = jnp.zeros(halo.shape, F32)

    def z_step(i, carry):
        for s in range(unroll):
            c = i * unroll + s
            slot = s
            ls = pl.ds(pl.multiple_of(c * wide, wide), wide)
            first, second = z0[:, ls], z1[:, ls]
            halo[slot, 0:2, :] = jnp.where(even_z, second, first)
            halo[slot, 2:4, :] = jnp.where(even_z, first, second)
            h = halo[slot]
            high = h.astype(jnp.bfloat16).astype(F32)
            both = jnp.concatenate([high, h - high], axis=0).astype(jnp.bfloat16)
            rhs[slot, 0:16, :] = both
            rhs[slot, 16:32, :] = both
            dz_v[:, ls] = z_own[:, ls] + jnp.dot(matrix[...], rhs[slot], preferred_element_type=F32)
            copy(dz_v, dz, sem_z, c).start()
        return carry

    lax.fori_loop(0, chunks // unroll, z_step, 0)

    y_low = jnp.where(even_y, y1[0:rows, :], y0[...]) * np.float32(EDGE)
    y_high = jnp.where(even_y, y0[...], y1[0:rows, :]) * np.float32(EDGE)
    s_low, s_high = y_low[:, :LANES], y_high[:, :LANES]
    state = u_v[:, 0:LANES] * np.float32(EDGE) + s_low * np.float32(ROOT - 1 / ROOT)

    def forward(i, state):
        for k in range(FORWARD):
            j = FORWARD * i + k
            state = v[j] + state * np.float32(ROOT)
            y[j] = state
        return state

    state = lax.fori_loop(0, points // FORWARD, forward, state) + s_high
    y[points - 1] = state
    u_last = rolled(u_v[:, width - LANES :], 96) * np.float32(EDGE)
    after = state * np.float32(ROOT) - u_last
    far = after * np.float32(ROOT) - s_high
    state = after + far * np.float32(ROOT / (1 - ROOT * ROOT))
    part = rows // 2
    lane = lane_index(part)
    state = [state[:part], state[part:]]
    for c in reversed(range(chunks)):
        for b in reversed(range(per)):
            for h in range(rows // part):
                rs = slice(h * part, (h + 1) * part)
                d = [None] * 4
                for k in reversed(range(4)):
                    j = 4 * (per * c + b) + k
                    state[h] = y[j, rs, :] + state[h] * np.float32(ROOT)
                    d[k] = v[j, rs, :] + state[h] * np.float32(-25 * ROOT)
                    if j == points - 1:
                        d[k] = d[k] + y_high[rs, LANES:]
                    if j == 0:
                        d[k] = d[k] - y_low[rs, LANES:]
                d1, d2, d3 = rolled(d[1], 96), rolled(d[2], 64), rolled(d[3], 32)
                at = c * wide + b * BLOCK
                for k, o in enumerate((jnp.where(lane < 96, d[0], d1), jnp.where(lane < 64, d1, d2), jnp.where(lane < 32, d2, d3))):
                    dy_v[rs, at + k * LANES : at + (k + 1) * LANES] = o
        copy(dy_v, dy, sem_y, c).start()

    for c in range(chunks):
        copy(dz_v, dz, sem_z, c).wait()
        copy(dy_v, dy, sem_y, c).wait()


VMEM = pl.BlockSpec(memory_space=pltpu.VMEM)
ANY = pl.BlockSpec(memory_space=pl.ANY)


def params(mib):
    return pltpu.CompilerParams(vmem_limit_bytes=mib * 1024 * 1024)


def here(x):
    return pltpu.with_memory_space_constraint(x, pltpu.VMEM)


def shards(velocity):
    rows, width = velocity.shape
    points = width // X
    chunks = 12
    whole = jax.ShapeDtypeStruct((rows, width), F32)
    matrix = jnp.asarray(z_matrix(rows))
    u_v, z0, z1, y0, y1, z_own, v = pl.pallas_call(
        functools.partial(summarize, chunks=chunks, unroll=UL),
        out_shape=(
            pltpu.VMEM((rows, width), F32),
            jax.ShapeDtypeStruct((2, width), F32),
            jax.ShapeDtypeStruct((2, width), F32),
            jax.ShapeDtypeStruct((rows, 2 * LANES), F32),
            jax.ShapeDtypeStruct((rows + 8, 2 * LANES), F32),
            pltpu.VMEM((rows, width), F32),
            pltpu.VMEM((points, rows, LANES), F32),
        ),
        in_specs=[ANY] * 2,
        out_specs=(VMEM,) * 7,
        scratch_shapes=[
            pltpu.VMEM((rows, BLOCK), F32),
            pltpu.VMEM((rows, BLOCK), F32),
            pltpu.VMEM((2 * rows, 2 * rows), jnp.bfloat16),
            pltpu.VMEM((UL, 2 * rows, width // chunks), jnp.bfloat16),
            pltpu.VMEM((rows, LANES), F32),
            pltpu.SemaphoreType.DMA((chunks + 1,)),
        ],
        compiler_params=params(12),
        name="summarize",
    )(pltpu.with_memory_space_constraint(velocity, pltpu.HBM), pltpu.with_memory_space_constraint(matrix, pltpu.HBM))

    def swap(x, axis, first):
        count = lax.axis_size(axis)
        pairs = [(i % count, (i + 1) % count) for i in range(first, count + first, 2)]
        return lax.ppermute(x, axis, pairs + [(b, a) for a, b in pairs])

    z1 = swap(z1, "gz", 1)
    z0 = swap(z0, "gz", 0)
    y0, y1 = swap(y0, "gy", 0), swap(y1, "gy", 1)
    z_own, v = pl.pallas_call(
        functools.partial(local, chunks=chunks, unroll=UL),
        out_shape=(pltpu.VMEM((rows, width), F32), pltpu.VMEM((points, rows, LANES), F32)),
        in_specs=[VMEM] * 4,
        out_specs=(VMEM,) * 2,
        input_output_aliases={2: 0, 3: 1},
        scratch_shapes=[pltpu.VMEM((UL, 2 * rows, width // chunks), jnp.bfloat16), pltpu.VMEM((rows, LANES), F32)],
        compiler_params=params(8),
        cost_estimate=pl.CostEstimate(flops=8_000_000, bytes_accessed=10_000_000, transcendentals=0),
        name="local",
    )(here(u_v), matrix, here(z_own), here(v))
    return pl.pallas_call(
        functools.partial(finish, chunks=chunks, unroll=UF),
        out_shape=(whole, whole),
        in_specs=[VMEM] * 8,
        out_specs=(ANY, ANY),
        scratch_shapes=[
            pltpu.VMEM((points, rows, LANES), F32),
            pltpu.VMEM((rows, width), F32),
            pltpu.VMEM((rows, width), F32),
            pltpu.VMEM((UF, 8, width // chunks), F32),
            pltpu.VMEM((UF, 32, width // chunks), jnp.bfloat16),
            pltpu.SemaphoreType.DMA((chunks,)),
            pltpu.SemaphoreType.DMA((chunks,)),
        ],
        compiler_params=params(26),
        cost_estimate=pl.CostEstimate(flops=8_000_000, bytes_accessed=14_000_000, transcendentals=0),
        name="finish",
    )(here(u_v), here(z_own), here(v), jnp.asarray(halo_matrix(rows)), z0, z1, y0, y1)


def solution(mesh):
    return jax.shard_map(
        shards,
        mesh=mesh,
        in_specs=(P("gz", "gy"),),
        out_specs=(P("gz", "gy"), P("gz", "gy")),
        check_vma=False,
    )
```

```python
import functools

import jax
import jax.numpy as jnp
import ml_dtypes
import numpy as np
from jax import lax
from jax.experimental import pallas as pl
from jax.experimental.pallas import tpu as pltpu
from jax.sharding import PartitionSpec as P

X = 96
ROOT = (5.0**0.5 - 3.0) / 2.0
EDGE = 1.0 / 12.0
GAIN = 25.0 / 12.0
LANES = 128
BLOCK = 4 * X
Q = ROOT**4
UL = 2
UF = 4
FORWARD = 48
F32 = jnp.float32


def lane_index(rows):
    return lax.broadcasted_iota(jnp.int32, (rows, LANES), 1)


def rolled(x, by):
    return pltpu.roll(x, by, 1)


def spread(d, lane):
    d1, d2, d3 = rolled(d[1], 96), rolled(d[2], 64), rolled(d[3], 32)
    return jnp.where(lane < 96, d[0], d1), jnp.where(lane < 64, d1, d2), jnp.where(lane < 32, d2, d3)


def apart(v0, v1, v2, lane):
    return [
        v0,
        rolled(jnp.where(lane < 96, v1, v0), 32),
        rolled(jnp.where(lane < 64, v2, v1), 64),
        rolled(v2, 96),
    ]


def is_even(axis):
    return lax.rem(lax.axis_index(axis), 2) == 0


def summarize(u_hbm, m_hbm, u_v, z0, z1, y1, y0, z_own, v, acc_f, acc_b, matrix, rhs, last, sems, *, chunks, unroll):
    rows, width = u_v.shape
    wide = width // chunks
    per = wide // BLOCK
    even_z, even_y = is_even("gz"), is_even("gy")

    def copy(c):
        lanes = pl.ds(c * wide, wide)
        return pltpu.make_async_copy(u_hbm.at[:, lanes], u_v.at[:, lanes], sems.at[c])

    for c in range(chunks):
        copy(c).start()
    fetch = pltpu.make_async_copy(m_hbm, matrix, sems.at[chunks])
    fetch.start()
    sub = lax.broadcasted_iota(jnp.int32, (8, wide), 0)
    w_f = jnp.zeros((8, wide), F32)
    w_b = jnp.zeros((8, wide), F32)
    for r in range(8):
        w_f = jnp.where(sub == r, np.float32(ROOT ** (7 - r)), w_f)
        w_b = jnp.where(sub == r, np.float32(ROOT**r), w_b)
    for c in range(chunks):
        copy(c).wait()
        z_f = z_b = None
        for g in range(rows // 8):
            rs = slice(8 * g, 8 * g + 8)
            x = u_v[rs, c * wide : (c + 1) * wide]
            if g == 0:
                z_f, z_b = x, x
            else:
                z_f = z_f * np.float32(ROOT**8) + x
                z_b = z_b + x * np.float32(ROOT ** (8 * g))
            parts = [x[:, b * BLOCK : (b + 1) * BLOCK] for b in range(per)]
            y_f = acc_f[rs, :] if c else None
            for part in parts:
                y_f = part if y_f is None else y_f * np.float32(Q) + part
            acc_f[rs, :] = y_f
            y_b = None
            for part in reversed(parts):
                y_b = part if y_b is None else y_b * np.float32(Q) + part
            acc_b[rs, :] = acc_b[rs, :] + y_b * np.float32(Q ** (per * c)) if c else y_b
        lanes = slice(c * wide, (c + 1) * wide)
        s_f = jnp.sum(z_f * w_f, axis=0, keepdims=True)
        s_b = jnp.sum(z_b * w_b, axis=0, keepdims=True)
        e_f, e_b = u_v[rows - 1 : rows, lanes], u_v[0:1, lanes]
        z0[0:1, lanes] = jnp.where(even_z, s_f, s_b)
        z1[0:1, lanes] = jnp.where(even_z, s_b, s_f)
        z0[1:2, lanes] = jnp.where(even_z, e_f, e_b)
        z1[1:2, lanes] = jnp.where(even_z, e_b, e_f)
    lane = lane_index(8)
    half = rows // 2

    def y_ends(rs):
        v0, v1, v2 = (acc_f[rs, k * LANES : (k + 1) * LANES] for k in range(3))
        s = v2 + np.float32(ROOT) * jnp.where(lane < 96, rolled(v1, 96), rolled(v2, 96))
        s = s + np.float32(ROOT**2) * jnp.where(lane < 64, rolled(v0, 64), rolled(v1, 64))
        s = s + np.float32(ROOT**3) * rolled(v0, 32)
        s_f, e_f = rolled(s, 96), rolled(u_v[rs, width - LANES :], 96)
        v0, v1, v2 = (acc_b[rs, k * LANES : (k + 1) * LANES] for k in range(3))
        s = v0 + np.float32(ROOT) * jnp.where(lane < 32, rolled(v0, 32), rolled(v1, 32))
        s = s + np.float32(ROOT**2) * jnp.where(lane < 64, rolled(v1, 64), rolled(v2, 64))
        s_b, e_b = s + np.float32(ROOT**3) * rolled(v2, 96), u_v[rs, 0:LANES]
        return (s_f, e_f), (s_b, e_b)

    for g in range(half // 8):
        f_0, b_0 = y_ends(slice(8 * g, 8 * g + 8))
        f_1, b_1 = y_ends(slice(half + 8 * g, half + 8 * g + 8))
        rs = slice(8 * g, 8 * g + 8)
        for k, (f, b) in enumerate(zip(spread(f_0 + f_1, lane), spread(b_0 + b_1, lane))):
            y0[rs, k * LANES : (k + 1) * LANES] = jnp.where(even_y, f, b)
            y1[rs, k * LANES : (k + 1) * LANES] = jnp.where(even_y, b, f)
    fetch.wait()

    @pl.when(at_wrap())
    def _():
        own_parts(u_v, matrix, z_own, v, rhs, last, chunks=chunks, unroll=unroll)


def halves(x):
    high = x.astype(jnp.bfloat16)
    return high, (x - high.astype(F32)).astype(jnp.bfloat16)


def z_matrix(rows):
    at = np.arange(rows)
    k = at[:, None] - at[None, :]
    own = GAIN * np.sign(k) * ROOT ** np.abs(k) - EDGE * ((k == 1).astype(float) - (k == -1))
    whole = np.concatenate([own, own], axis=1).astype(np.float32)
    high = whole.astype(ml_dtypes.bfloat16)
    low = (whole - high.astype(np.float32)).astype(ml_dtypes.bfloat16)
    return np.concatenate([high, low], axis=0)


def own_parts(u_v, matrix, z_own, v, rhs, last, *, chunks, unroll):
    rows, width = u_v.shape
    wide = width // chunks
    per = wide // BLOCK
    part = rows // 4
    lane = lane_index(part)
    last[...] = jnp.zeros((rows, LANES), F32)

    for c in range(chunks):
        ls = slice(c * wide, (c + 1) * wide)
        slot = c % unroll
        rhs[slot, 0:rows, :], rhs[slot, rows:, :] = halves(u_v[:, ls])
        out = jnp.dot(matrix[...], rhs[slot], preferred_element_type=F32)
        z_own[:, ls] = out[:rows] + out[rows:]
        for r in range(0, rows, part):
            rs = slice(r, r + part)
            points = [last[rs, :]]
            for b in range(per):
                at = c * wide + b * BLOCK
                v0, v1, v2 = (u_v[rs, at + k * LANES : at + (k + 1) * LANES] * np.float32(EDGE) for k in range(3))
                points += apart(v0, v1, v2, lane)
            last[rs, :] = points[-1]
            if c < chunks - 1:
                points.append(u_v[rs, (c + 1) * wide : (c + 1) * wide + LANES] * np.float32(EDGE))
            else:
                points.append(jnp.zeros((part, LANES), F32))
            for k in range(4 * per):
                v[4 * per * c + k, rs, :] = points[k + 2] - points[k]


def at_wrap():
    return lax.axis_index("gz") == 0


def local(u_v, matrix, z_before, v_before, z_own, v, rhs, last, *, chunks, unroll):
    del z_before, v_before

    @pl.when(jnp.logical_not(at_wrap()))
    def _():
        own_parts(u_v, matrix, z_own, v, rhs, last, chunks=chunks, unroll=unroll)


def halo_matrix(rows):
    at = np.arange(rows)
    whole = np.zeros((rows, 8))
    whole[:, 0] = GAIN * ROOT ** (at + 1.0)
    whole[0, 1] = -EDGE
    whole[:, 2] = -GAIN * ROOT ** (rows - at * 1.0)
    whole[rows - 1, 3] = EDGE
    whole = whole.astype(np.float32)
    high = whole.astype(ml_dtypes.bfloat16)
    low = (whole - high.astype(np.float32)).astype(ml_dtypes.bfloat16)
    return np.concatenate([high, high, low, low], axis=1)


def finish(u_v, z_own, v, matrix, z0, z1, y1, y0, dy, dz, y, dy_v, dz_v, halo, rhs, sem_y, sem_z, *, chunks, unroll):
    rows, width = u_v.shape
    points = v.shape[0]
    wide = width // chunks
    per = wide // BLOCK
    even_z, even_y = is_even("gz"), is_even("gy")

    def copy(buffer, out, sems, c):
        ls = pl.ds(pl.multiple_of(c * wide, wide), wide)
        return pltpu.make_async_copy(buffer.at[:, ls], out.at[:, ls], sems.at[c])

    halo[...] = jnp.zeros(halo.shape, F32)

    def z_step(i, carry):
        for s in range(unroll):
            c = i * unroll + s
            slot = s
            ls = pl.ds(pl.multiple_of(c * wide, wide), wide)
            first, second = z0[:, ls], z1[:, ls]
            halo[slot, 0:2, :] = jnp.where(even_z, second, first)
            halo[slot, 2:4, :] = jnp.where(even_z, first, second)
            h = halo[slot]
            high = h.astype(jnp.bfloat16).astype(F32)
            both = jnp.concatenate([high, h - high], axis=0).astype(jnp.bfloat16)
            rhs[slot, 0:16, :] = both
            rhs[slot, 16:32, :] = both
            dz_v[:, ls] = z_own[:, ls] + jnp.dot(matrix[...], rhs[slot], preferred_element_type=F32)
            copy(dz_v, dz, sem_z, c).start()
        return carry

    lax.fori_loop(0, chunks // unroll, z_step, 0)

    part = rows // 2
    lane = lane_index(part)

    def y_halo(block):
        s_0, e_0, s_1, e_1 = apart(*(block[:, k * LANES : (k + 1) * LANES] * np.float32(EDGE) for k in range(3)), lane)
        return jnp.concatenate([s_0, s_1], axis=0), (e_0, e_1)

    s_low, e_low = y_halo(jnp.where(even_y, y1[...], y0[...]))
    s_high, e_high = y_halo(jnp.where(even_y, y0[...], y1[...]))
    state = u_v[:, 0:LANES] * np.float32(EDGE) + s_low * np.float32(ROOT - 1 / ROOT)

    def forward(i, state):
        for k in range(FORWARD):
            j = FORWARD * i + k
            state = v[j] + state * np.float32(ROOT)
            y[j] = state
        return state

    state = lax.fori_loop(0, points // FORWARD, forward, state) + s_high
    y[points - 1] = state
    u_last = rolled(u_v[:, width - LANES :], 96) * np.float32(EDGE)
    after = state * np.float32(ROOT) - u_last
    far = after * np.float32(ROOT) - s_high
    state = after + far * np.float32(ROOT / (1 - ROOT * ROOT))
    state = [state[:part], state[part:]]
    for c in reversed(range(chunks)):
        for b in reversed(range(per)):
            for h in range(rows // part):
                rs = slice(h * part, (h + 1) * part)
                d = [None] * 4
                for k in reversed(range(4)):
                    j = 4 * (per * c + b) + k
                    state[h] = y[j, rs, :] + state[h] * np.float32(ROOT)
                    d[k] = v[j, rs, :] + state[h] * np.float32(-25 * ROOT)
                    if j == points - 1:
                        d[k] = d[k] + e_high[h]
                    if j == 0:
                        d[k] = d[k] - e_low[h]
                at = c * wide + b * BLOCK
                for k, o in enumerate(spread(d, lane)):
                    dy_v[rs, at + k * LANES : at + (k + 1) * LANES] = o
        copy(dy_v, dy, sem_y, c).start()

    for c in range(chunks):
        copy(dz_v, dz, sem_z, c).wait()
        copy(dy_v, dy, sem_y, c).wait()


VMEM = pl.BlockSpec(memory_space=pltpu.VMEM)
ANY = pl.BlockSpec(memory_space=pl.ANY)


def params(mib):
    return pltpu.CompilerParams(vmem_limit_bytes=mib * 1024 * 1024)


def here(x):
    return pltpu.with_memory_space_constraint(x, pltpu.VMEM)


def shards(velocity):
    rows, width = velocity.shape
    points = width // X
    chunks = 12
    whole = jax.ShapeDtypeStruct((rows, width), F32)
    matrix = jnp.asarray(z_matrix(rows))
    u_v, z0, z1, y1, y0, z_own, v = pl.pallas_call(
        functools.partial(summarize, chunks=chunks, unroll=UL),
        out_shape=(
            pltpu.VMEM((rows, width), F32),
            jax.ShapeDtypeStruct((2, width), F32),
            jax.ShapeDtypeStruct((2, width), F32),
            jax.ShapeDtypeStruct((rows // 2, BLOCK), F32),
            jax.ShapeDtypeStruct((rows // 2, BLOCK), F32),
            pltpu.VMEM((rows, width), F32),
            pltpu.VMEM((points, rows, LANES), F32),
        ),
        in_specs=[ANY] * 2,
        out_specs=(VMEM,) * 7,
        scratch_shapes=[
            pltpu.VMEM((rows, BLOCK), F32),
            pltpu.VMEM((rows, BLOCK), F32),
            pltpu.VMEM((2 * rows, 2 * rows), jnp.bfloat16),
            pltpu.VMEM((UL, 2 * rows, width // chunks), jnp.bfloat16),
            pltpu.VMEM((rows, LANES), F32),
            pltpu.SemaphoreType.DMA((chunks + 1,)),
        ],
        compiler_params=params(12),
        name="summarize",
    )(pltpu.with_memory_space_constraint(velocity, pltpu.HBM), pltpu.with_memory_space_constraint(matrix, pltpu.HBM))

    def swap(x, axis, first):
        count = lax.axis_size(axis)
        pairs = [(i % count, (i + 1) % count) for i in range(first, count + first, 2)]
        return lax.ppermute(x, axis, pairs + [(b, a) for a, b in pairs])

    z1 = swap(z1, "gz", 1)
    z0 = swap(z0, "gz", 0)
    y0, y1 = swap(y0, "gy", 0), swap(y1, "gy", 1)
    z_own, v = pl.pallas_call(
        functools.partial(local, chunks=chunks, unroll=UL),
        out_shape=(pltpu.VMEM((rows, width), F32), pltpu.VMEM((points, rows, LANES), F32)),
        in_specs=[VMEM] * 4,
        out_specs=(VMEM,) * 2,
        input_output_aliases={2: 0, 3: 1},
        scratch_shapes=[pltpu.VMEM((UL, 2 * rows, width // chunks), jnp.bfloat16), pltpu.VMEM((rows, LANES), F32)],
        compiler_params=params(8),
        cost_estimate=pl.CostEstimate(flops=8_000_000, bytes_accessed=10_000_000, transcendentals=0),
        name="local",
    )(here(u_v), matrix, here(z_own), here(v))
    return pl.pallas_call(
        functools.partial(finish, chunks=chunks, unroll=UF),
        out_shape=(whole, whole),
        in_specs=[VMEM] * 8,
        out_specs=(ANY, ANY),
        scratch_shapes=[
            pltpu.VMEM((points, rows, LANES), F32),
            pltpu.VMEM((rows, width), F32),
            pltpu.VMEM((rows, width), F32),
            pltpu.VMEM((UF, 8, width // chunks), F32),
            pltpu.VMEM((UF, 32, width // chunks), jnp.bfloat16),
            pltpu.SemaphoreType.DMA((chunks,)),
            pltpu.SemaphoreType.DMA((chunks,)),
        ],
        compiler_params=params(26),
        cost_estimate=pl.CostEstimate(flops=8_000_000, bytes_accessed=14_000_000, transcendentals=0),
        name="finish",
    )(here(u_v), here(z_own), here(v), jnp.asarray(halo_matrix(rows)), z0, z1, y1, y0)


def solution(mesh):
    return jax.shard_map(
        shards,
        mesh=mesh,
        in_specs=(P("gz", "gy"),),
        out_specs=(P("gz", "gy"), P("gz", "gy")),
        check_vma=False,
    )
```

```python
import functools

import jax
import jax.numpy as jnp
import ml_dtypes
import numpy as np
from jax import lax
from jax.experimental import pallas as pl
from jax.experimental.pallas import tpu as pltpu
from jax.sharding import PartitionSpec as P

X = 96
ROOT = (5.0**0.5 - 3.0) / 2.0
EDGE = 1.0 / 12.0
GAIN = 25.0 / 12.0
LANES = 128
BLOCK = 4 * X
Q = ROOT**4
UL = 2
UF = 6
FORWARD = 48
F32 = jnp.float32


def lane_index(rows):
    return lax.broadcasted_iota(jnp.int32, (rows, LANES), 1)


def rolled(x, by):
    return pltpu.roll(x, by, 1)


def spread(d, lane):
    d1, d2, d3 = rolled(d[1], 96), rolled(d[2], 64), rolled(d[3], 32)
    return jnp.where(lane < 96, d[0], d1), jnp.where(lane < 64, d1, d2), jnp.where(lane < 32, d2, d3)


def apart(v0, v1, v2, lane):
    return [
        v0,
        rolled(jnp.where(lane < 96, v1, v0), 32),
        rolled(jnp.where(lane < 64, v2, v1), 64),
        rolled(v2, 96),
    ]


def is_even(axis):
    return lax.rem(lax.axis_index(axis), 2) == 0


def summarize(u_hbm, m_hbm, u_v, z0, z1, y1, y0, z_own, v, acc_f, acc_b, matrix, rhs, last, sems, *, chunks, unroll):
    rows, width = u_v.shape
    wide = width // chunks
    per = wide // BLOCK
    even_z, even_y = is_even("gz"), is_even("gy")

    def copy(c):
        lanes = pl.ds(c * wide, wide)
        return pltpu.make_async_copy(u_hbm.at[:, lanes], u_v.at[:, lanes], sems.at[c])

    for c in range(chunks):
        copy(c).start()
    fetch = pltpu.make_async_copy(m_hbm, matrix, sems.at[chunks])
    fetch.start()
    sub = lax.broadcasted_iota(jnp.int32, (8, wide), 0)
    w_f = jnp.zeros((8, wide), F32)
    w_b = jnp.zeros((8, wide), F32)
    for r in range(8):
        w_f = jnp.where(sub == r, np.float32(ROOT ** (7 - r)), w_f)
        w_b = jnp.where(sub == r, np.float32(ROOT**r), w_b)
    for c in range(chunks):
        copy(c).wait()
        z_f = z_b = None
        for g in range(rows // 8):
            rs = slice(8 * g, 8 * g + 8)
            x = u_v[rs, c * wide : (c + 1) * wide]
            if g == 0:
                z_f, z_b = x, x
            else:
                z_f = z_f * np.float32(ROOT**8) + x
                z_b = z_b + x * np.float32(ROOT ** (8 * g))
            parts = [x[:, b * BLOCK : (b + 1) * BLOCK] for b in range(per)]
            y_f = acc_f[rs, :] if c else None
            for part in parts:
                y_f = part if y_f is None else y_f * np.float32(Q) + part
            acc_f[rs, :] = y_f
            y_b = None
            for part in reversed(parts):
                y_b = part if y_b is None else y_b * np.float32(Q) + part
            acc_b[rs, :] = acc_b[rs, :] + y_b * np.float32(Q ** (per * c)) if c else y_b
        lanes = slice(c * wide, (c + 1) * wide)
        s_f = jnp.sum(z_f * w_f, axis=0, keepdims=True)
        s_b = jnp.sum(z_b * w_b, axis=0, keepdims=True)
        e_f, e_b = u_v[rows - 1 : rows, lanes], u_v[0:1, lanes]
        z0[0:1, lanes] = jnp.where(even_z, s_f, s_b)
        z1[0:1, lanes] = jnp.where(even_z, s_b, s_f)
        z0[1:2, lanes] = jnp.where(even_z, e_f, e_b)
        z1[1:2, lanes] = jnp.where(even_z, e_b, e_f)
    lane = lane_index(8)
    half = rows // 2

    def y_ends(rs):
        v0, v1, v2 = (acc_f[rs, k * LANES : (k + 1) * LANES] for k in range(3))
        s = v2 + np.float32(ROOT) * jnp.where(lane < 96, rolled(v1, 96), rolled(v2, 96))
        s = s + np.float32(ROOT**2) * jnp.where(lane < 64, rolled(v0, 64), rolled(v1, 64))
        s = s + np.float32(ROOT**3) * rolled(v0, 32)
        s_f, e_f = rolled(s, 96), rolled(u_v[rs, width - LANES :], 96)
        v0, v1, v2 = (acc_b[rs, k * LANES : (k + 1) * LANES] for k in range(3))
        s = v0 + np.float32(ROOT) * jnp.where(lane < 32, rolled(v0, 32), rolled(v1, 32))
        s = s + np.float32(ROOT**2) * jnp.where(lane < 64, rolled(v1, 64), rolled(v2, 64))
        s_b, e_b = s + np.float32(ROOT**3) * rolled(v2, 96), u_v[rs, 0:LANES]
        return (s_f, e_f), (s_b, e_b)

    for g in range(half // 8):
        f_0, b_0 = y_ends(slice(8 * g, 8 * g + 8))
        f_1, b_1 = y_ends(slice(half + 8 * g, half + 8 * g + 8))
        rs = slice(8 * g, 8 * g + 8)
        for k, (f, b) in enumerate(zip(spread(f_0 + f_1, lane), spread(b_0 + b_1, lane))):
            y0[rs, k * LANES : (k + 1) * LANES] = jnp.where(even_y, f, b)
            y1[rs, k * LANES : (k + 1) * LANES] = jnp.where(even_y, b, f)
    fetch.wait()

    @pl.when(at_wrap())
    def _():
        own_parts(u_v, matrix, z_own, v, rhs, last, chunks=chunks, unroll=unroll)


def halves(x):
    high = x.astype(jnp.bfloat16)
    return high, (x - high.astype(F32)).astype(jnp.bfloat16)


def z_matrix(rows):
    at = np.arange(rows)
    k = at[:, None] - at[None, :]
    own = GAIN * np.sign(k) * ROOT ** np.abs(k) - EDGE * ((k == 1).astype(float) - (k == -1))
    whole = np.concatenate([own, own], axis=1).astype(np.float32)
    high = whole.astype(ml_dtypes.bfloat16)
    low = (whole - high.astype(np.float32)).astype(ml_dtypes.bfloat16)
    return np.concatenate([high, low], axis=0)


def own_parts(u_v, matrix, z_own, v, rhs, last, *, chunks, unroll):
    rows, width = u_v.shape
    wide = width // chunks
    per = wide // BLOCK
    part = rows // 4
    lane = lane_index(part)
    last[...] = jnp.zeros((rows, LANES), F32)

    for c in range(chunks):
        ls = slice(c * wide, (c + 1) * wide)
        slot = c % unroll
        rhs[slot, 0:rows, :], rhs[slot, rows:, :] = halves(u_v[:, ls])
        out = jnp.dot(matrix[...], rhs[slot], preferred_element_type=F32)
        z_own[:, ls] = out[:rows] + out[rows:]
        for r in range(0, rows, part):
            rs = slice(r, r + part)
            points = [last[rs, :]]
            for b in range(per):
                at = c * wide + b * BLOCK
                v0, v1, v2 = (u_v[rs, at + k * LANES : at + (k + 1) * LANES] * np.float32(EDGE) for k in range(3))
                points += apart(v0, v1, v2, lane)
            last[rs, :] = points[-1]
            if c < chunks - 1:
                points.append(u_v[rs, (c + 1) * wide : (c + 1) * wide + LANES] * np.float32(EDGE))
            else:
                points.append(jnp.zeros((part, LANES), F32))
            for k in range(4 * per):
                v[4 * per * c + k, rs, :] = points[k + 2] - points[k]


def at_wrap():
    return lax.axis_index("gz") == 0


def local(u_v, matrix, z_before, v_before, z_own, v, rhs, last, *, chunks, unroll):
    del z_before, v_before

    @pl.when(jnp.logical_not(at_wrap()))
    def _():
        own_parts(u_v, matrix, z_own, v, rhs, last, chunks=chunks, unroll=unroll)


def halo_matrix(rows):
    at = np.arange(rows)
    whole = np.zeros((rows, 8))
    whole[:, 0] = GAIN * ROOT ** (at + 1.0)
    whole[0, 1] = -EDGE
    whole[:, 2] = -GAIN * ROOT ** (rows - at * 1.0)
    whole[rows - 1, 3] = EDGE
    whole = whole.astype(np.float32)
    high = whole.astype(ml_dtypes.bfloat16)
    low = (whole - high.astype(np.float32)).astype(ml_dtypes.bfloat16)
    return np.concatenate([high, high, low, low], axis=1)


def finish(u_v, z_own, v, matrix, z0, z1, y1, y0, dy, dz, y, dy_v, dz_v, halo, rhs, sem_y, sem_z, *, chunks, unroll):
    rows, width = u_v.shape
    points = v.shape[0]
    wide = width // chunks
    per = wide // BLOCK
    even_z, even_y = is_even("gz"), is_even("gy")

    def copy(buffer, out, sems, c):
        ls = pl.ds(pl.multiple_of(c * wide, wide), wide)
        return pltpu.make_async_copy(buffer.at[:, ls], out.at[:, ls], sems.at[c])

    halo[...] = jnp.zeros(halo.shape, F32)

    def z_step(i, carry):
        for s in range(unroll):
            c = i * unroll + s
            slot = s
            ls = pl.ds(pl.multiple_of(c * wide, wide), wide)
            first, second = z0[:, ls], z1[:, ls]
            halo[slot, 0:2, :] = jnp.where(even_z, second, first)
            halo[slot, 2:4, :] = jnp.where(even_z, first, second)
            h = halo[slot]
            high = h.astype(jnp.bfloat16).astype(F32)
            both = jnp.concatenate([high, h - high], axis=0).astype(jnp.bfloat16)
            rhs[slot, 0:16, :] = both
            rhs[slot, 16:32, :] = both
            dz_v[:, ls] = z_own[:, ls] + jnp.dot(matrix[...], rhs[slot], preferred_element_type=F32)
            copy(dz_v, dz, sem_z, c).start()
        return carry

    lax.fori_loop(0, chunks // unroll, z_step, 0)

    part = rows // 2
    lane = lane_index(part)

    def y_halo(block):
        s_0, e_0, s_1, e_1 = apart(*(block[:, k * LANES : (k + 1) * LANES] * np.float32(EDGE) for k in range(3)), lane)
        return jnp.concatenate([s_0, s_1], axis=0), (e_0, e_1)

    s_low, e_low = y_halo(jnp.where(even_y, y1[...], y0[...]))
    s_high, e_high = y_halo(jnp.where(even_y, y0[...], y1[...]))
    state = u_v[:, 0:LANES] * np.float32(EDGE) + s_low * np.float32(ROOT - 1 / ROOT)

    def forward(i, state):
        for k in range(FORWARD):
            j = FORWARD * i + k
            state = v[j] + state * np.float32(ROOT)
            y[j] = state
        return state

    state = lax.fori_loop(0, points // FORWARD, forward, state) + s_high
    y[points - 1] = state
    u_last = rolled(u_v[:, width - LANES :], 96) * np.float32(EDGE)
    after = state * np.float32(ROOT) - u_last
    far = after * np.float32(ROOT) - s_high
    state = after + far * np.float32(ROOT / (1 - ROOT * ROOT))
    state = [state[:part], state[part:]]
    for c in reversed(range(chunks)):
        for b in reversed(range(per)):
            for h in range(rows // part):
                rs = slice(h * part, (h + 1) * part)
                d = [None] * 4
                for k in reversed(range(4)):
                    j = 4 * (per * c + b) + k
                    state[h] = y[j, rs, :] + state[h] * np.float32(ROOT)
                    d[k] = v[j, rs, :] + state[h] * np.float32(-25 * ROOT)
                    if j == points - 1:
                        d[k] = d[k] + e_high[h]
                    if j == 0:
                        d[k] = d[k] - e_low[h]
                at = c * wide + b * BLOCK
                for k, o in enumerate(spread(d, lane)):
                    dy_v[rs, at + k * LANES : at + (k + 1) * LANES] = o
        copy(dy_v, dy, sem_y, c).start()

    for c in range(chunks):
        copy(dz_v, dz, sem_z, c).wait()
        copy(dy_v, dy, sem_y, c).wait()


VMEM = pl.BlockSpec(memory_space=pltpu.VMEM)
ANY = pl.BlockSpec(memory_space=pl.ANY)


def params(mib):
    return pltpu.CompilerParams(vmem_limit_bytes=mib * 1024 * 1024)


def here(x):
    return pltpu.with_memory_space_constraint(x, pltpu.VMEM)


def shards(velocity):
    rows, width = velocity.shape
    points = width // X
    chunks = 12
    whole = jax.ShapeDtypeStruct((rows, width), F32)
    matrix = jnp.asarray(z_matrix(rows))
    u_v, z0, z1, y1, y0, z_own, v = pl.pallas_call(
        functools.partial(summarize, chunks=chunks, unroll=UL),
        out_shape=(
            pltpu.VMEM((rows, width), F32),
            jax.ShapeDtypeStruct((2, width), F32),
            jax.ShapeDtypeStruct((2, width), F32),
            jax.ShapeDtypeStruct((rows // 2, BLOCK), F32),
            jax.ShapeDtypeStruct((rows // 2, BLOCK), F32),
            pltpu.VMEM((rows, width), F32),
            pltpu.VMEM((points, rows, LANES), F32),
        ),
        in_specs=[ANY] * 2,
        out_specs=(VMEM,) * 7,
        scratch_shapes=[
            pltpu.VMEM((rows, BLOCK), F32),
            pltpu.VMEM((rows, BLOCK), F32),
            pltpu.VMEM((2 * rows, 2 * rows), jnp.bfloat16),
            pltpu.VMEM((UL, 2 * rows, width // chunks), jnp.bfloat16),
            pltpu.VMEM((rows, LANES), F32),
            pltpu.SemaphoreType.DMA((chunks + 1,)),
        ],
        compiler_params=params(12),
        name="summarize",
    )(pltpu.with_memory_space_constraint(velocity, pltpu.HBM), pltpu.with_memory_space_constraint(matrix, pltpu.HBM))

    def swap(x, axis, first):
        count = lax.axis_size(axis)
        pairs = [(i % count, (i + 1) % count) for i in range(first, count + first, 2)]
        return lax.ppermute(x, axis, pairs + [(b, a) for a, b in pairs])

    z1 = swap(z1, "gz", 1)
    z0 = swap(z0, "gz", 0)
    y0, y1 = swap(y0, "gy", 0), swap(y1, "gy", 1)
    z_own, v = pl.pallas_call(
        functools.partial(local, chunks=chunks, unroll=UL),
        out_shape=(pltpu.VMEM((rows, width), F32), pltpu.VMEM((points, rows, LANES), F32)),
        in_specs=[VMEM] * 4,
        out_specs=(VMEM,) * 2,
        input_output_aliases={2: 0, 3: 1},
        scratch_shapes=[pltpu.VMEM((UL, 2 * rows, width // chunks), jnp.bfloat16), pltpu.VMEM((rows, LANES), F32)],
        compiler_params=params(8),
        cost_estimate=pl.CostEstimate(flops=8_000_000, bytes_accessed=10_000_000, transcendentals=0),
        name="local",
    )(here(u_v), matrix, here(z_own), here(v))
    return pl.pallas_call(
        functools.partial(finish, chunks=chunks, unroll=UF),
        out_shape=(whole, whole),
        in_specs=[VMEM] * 8,
        out_specs=(ANY, ANY),
        scratch_shapes=[
            pltpu.VMEM((points, rows, LANES), F32),
            pltpu.VMEM((rows, width), F32),
            pltpu.VMEM((rows, width), F32),
            pltpu.VMEM((UF, 8, width // chunks), F32),
            pltpu.VMEM((UF, 32, width // chunks), jnp.bfloat16),
            pltpu.SemaphoreType.DMA((chunks,)),
            pltpu.SemaphoreType.DMA((chunks,)),
        ],
        compiler_params=params(26),
        cost_estimate=pl.CostEstimate(flops=8_000_000, bytes_accessed=14_000_000, transcendentals=0),
        name="finish",
    )(here(u_v), here(z_own), here(v), jnp.asarray(halo_matrix(rows)), z0, z1, y1, y0)


def solution(mesh):
    return jax.shard_map(
        shards,
        mesh=mesh,
        in_specs=(P("gz", "gy"),),
        out_specs=(P("gz", "gy"), P("gz", "gy")),
        check_vma=False,
    )
```
